768 devices in a mesh: rep: 48 (over z, x_lo, core), blk: 16 (over y, x_hi).
Axes of the slice: x: 4 (x_hi: 2, x_lo: 2; x = x_hi * 2 + x_lo), y: 8, z: 12, core: 2. Of those that a mesh axis runs over, the one named last changes fastest.
Arguments:
- features: bfloat16 [98304, 128], P(('rep', 'blk')), may hold values from -6 to 6
- weight: bfloat16 [128, 128], replicated, may hold values from -0.5 to 0.5
- bias: float32 [128], replicated, may hold values from -3 to 3
- tile_vals: bfloat16 [48, 16, 128, 128, 128], P('rep', 'blk'), may hold values from -0.078125 to 0.078125
- tile_pos: int32 [48, 16, 128], P('rep', 'blk'), may hold values from 0 to 47
- tile_counts: int32 [48, 16, 16], P('rep', 'blk'), may hold values from 1 to 8, as said below
- grad_out: bfloat16 [98304, 128], P(('rep', 'blk')), may hold values from -6 to 6
Outputs:
- activations: bfloat16 [98304, 128], P(('rep', 'blk'))
- grad_weight: float32 [128, 128], replicated
- grad_features: bfloat16 [98304, 128], P(('rep', 'blk'))
The draws below stay inside these ranges and needn't reach their ends.
Inputs may be any that keep to these rules, and one draw needn't show every extreme that they name: `tile_counts`: on every device some column block has all 8 slots live.
All inputs are finite; a program needn't handle non-finite values.
Results may differ from the reference program's by a relative error of at most 0.02.
Values may be sent and summed in bfloat16 or wider, within the bound.
No kernel may reach another device: no remote copies, remote signals or barrier semaphores. Data moves between devices by JAX's collectives and lax.ppermute only.
A program may use at most 64 MiB of HBM per device.

```python
import jax
import jax.numpy as jnp
from jax import lax

F = 128
H = 128
TILE = 128
RT = 1
SLOTS = 8
NODES = 98304
N_REP = 48
N_BLK = 16


def draw_tile_counts(key, part):
    key = jax.random.fold_in(key, 11)
    key_level, key_base, key_full = jax.random.split(key, 3)
    level = jax.random.randint(key_level, (N_REP, N_BLK, 1), 1, 5)
    base = jax.random.randint(key_base, (N_REP, N_BLK, N_BLK), 1, SLOTS + 1)
    counts = jnp.maximum(1, base * level // 4)
    full_block = jax.random.randint(key_full, (N_REP, N_BLK, 1), 0, N_BLK)
    block_ids = jnp.arange(N_BLK, dtype=jnp.int32)[None, None, :]
    counts = jnp.where(block_ids == full_block, SLOTS, counts)
    return counts.astype(jnp.int32)


def plant(array, key, least, largest):
    longest = array.shape.index(max(array.shape))
    spots = []
    for shift in (0, 1):
        where = [jax.random.randint(jax.random.fold_in(key, axis), (), 0, length) for axis, length in enumerate(array.shape)]
        where[longest] = (where[longest] + shift) % array.shape[longest]
        spots.append(tuple(where))
    return array.at[spots[0]].set(least).at[spots[1]].set(largest)


def steps_of(rng, shape, cuts, low, top_value):
    factor_of, own = 1.0, jax.random.fold_in(rng, 6)
    for dim, blocks in cuts:
        heights = jnp.exp(jax.random.uniform(jax.random.fold_in(own, dim), (blocks,), jnp.float32, low / len(cuts), top_value / len(cuts)))
        factor_of = factor_of * jnp.repeat(heights, shape[dim] // blocks).reshape([-1 if axis == dim else 1 for axis in range(len(shape))])
    return factor_of


def gaussian(stream_key, shape, scale, limit, cuts=(), kind=jnp.bfloat16):
    result = jax.random.normal(stream_key, shape, jnp.float32) * scale
    if len(cuts) > 0:
        result = steps_of(stream_key, shape, cuts, -0.22, 0.18) * result
    return jnp.clip(result, min=-limit, max=limit).astype(kind)


def setup_inputs(seed: int = 0) -> dict:
    keys = jax.random.split(jax.random.key(seed), 8)
    features = gaussian(keys[0], (NODES, F), 1.0, 6.0, ((0, 768),))
    weight = gaussian(keys[1], (F, H), F ** -0.5, 0.5)
    bias = gaussian(keys[2], (H,), 0.5, 3.0, (), jnp.float32)
    tile_vals = gaussian(keys[3], (N_REP, N_BLK, N_BLK * SLOTS, TILE, TILE), (TILE * N_BLK * SLOTS // (3 * RT)) ** -0.5, 0.078125, ((0, 48), (1, 16)))
    tile_pos = plant(jax.random.randint(keys[4], (N_REP, N_BLK, N_BLK * SLOTS), 0, N_REP * RT * RT), jax.random.fold_in(keys[4], 1), 0, (N_REP * RT * RT) - 1).astype(jnp.int32)
    tile_counts = draw_tile_counts(jax.random.fold_in(keys[7], 71), 0)
    grad_out = gaussian(keys[6], (NODES, H), 1.0, 6.0, ((0, 768),))
    return dict(features=features, weight=weight, bias=bias, tile_vals=tile_vals, tile_pos=tile_pos, tile_counts=tile_counts, grad_out=grad_out)


def reference(features, weight, bias, tile_vals, tile_pos, tile_counts, grad_out):
    slot_ids = jnp.arange(N_BLK * SLOTS, dtype=jnp.int32)
    block_of = (slot_ids // SLOTS).astype(jnp.int32)
    live_slots = (slot_ids % SLOTS)[None, None, :] < tile_counts[:, :, block_of]
    row_tile = tile_pos // RT
    col_tile = tile_pos % RT
    dest_rep = row_tile // RT
    dest_part = row_tile % RT
    block_ids = jnp.arange(N_BLK, dtype=jnp.int32)[:, None]
    feature_tiles = features.reshape(N_REP, N_BLK, RT, TILE, F)

    def forward_step(running, replica):
        sources = feature_tiles[replica][block_of[None, :], col_tile[replica]]
        products = jnp.einsum('bkac,bkcf->bkaf', tile_vals[replica].astype(jnp.float32), sources.astype(jnp.float32))
        products = jnp.where(live_slots[replica][:, :, None, None], products, jnp.float32(0.0))
        running = running.at[dest_rep[replica], block_ids, dest_part[replica]].add(products)
        return (running, None)
    start_sum = jnp.zeros((N_REP, N_BLK, RT, TILE, F), jnp.float32)
    aggregate, unused = lax.scan(forward_step, start_sum, jnp.arange(N_REP, dtype=jnp.int32))
    aggregate_bf = aggregate.reshape(NODES, F).astype(jnp.bfloat16)
    pre = jnp.dot(aggregate_bf, weight, preferred_element_type=jnp.float32) + bias
    activations = jax.nn.elu(pre).astype(jnp.bfloat16)
    slope = jnp.where(pre > 0, jnp.float32(1.0), jnp.exp(jnp.minimum(pre, jnp.float32(0.0))))
    grad_pre = (grad_out.astype(jnp.float32) * slope).astype(jnp.bfloat16)
    grad_weight = jnp.dot(aggregate_bf.T, grad_pre, preferred_element_type=jnp.float32) / jnp.sqrt(jnp.float32(NODES))
    grad_rows = jnp.dot(grad_pre, weight.T, preferred_element_type=jnp.float32).astype(jnp.bfloat16)
    gradient_tiles = grad_rows.reshape(N_REP, N_BLK, RT, TILE, F)

    def backward_step(replica):
        sources = gradient_tiles[dest_rep[replica], block_ids, dest_part[replica]]
        products = jnp.einsum('bkac,bkaf->bkcf', tile_vals[replica].astype(jnp.float32), sources.astype(jnp.float32))
        products = jnp.where(live_slots[replica][:, :, None, None], products, jnp.float32(0.0))
        columns = jnp.zeros((N_BLK, RT, TILE, F), jnp.float32)
        return columns.at[block_of[None, :], col_tile[replica]].add(products)
    grad_tiles = lax.map(backward_step, jnp.arange(N_REP, dtype=jnp.int32))
    grad_features = grad_tiles.reshape(NODES, F).astype(jnp.bfloat16)
    return (activations, grad_weight, grad_features)
```

```python
import functools
import math

import jax
import jax.numpy as jnp
from jax import lax
from jax.experimental import pallas as pl
from jax.experimental.pallas import tpu as pltpu
from jax.sharding import Mesh, PartitionSpec as P

AXES = ("z", "x_lo", "core", "y", "x_hi")
REP = ("z", "x_lo", "core")
BLK = ("y", "x_hi")
BF16 = jnp.bfloat16
F32 = jnp.float32
VMEM = pl.BlockSpec(memory_space=pltpu.VMEM)
SMEM = pl.BlockSpec(memory_space=pltpu.SMEM)
LIMIT = 24 * 1024 * 1024


def place_of(pos, mine, z_count):
    differs = pos ^ mine
    return ((differs & 1) * 2 + ((differs >> 1) & 1)) * z_count + (pos >> 2)


def forward_kernel(z_count, slots, mine_ref, pos_ref, counts_ref, tiles_ref, rows_ref, send_ref, keep_ref, acc_ref):
    blocks, tile, width = rows_ref.shape
    half = 2 * z_count
    acc_ref[...] = jnp.zeros_like(acc_ref)
    mine = mine_ref[0]

    def block_step(j, carry):
        base = j * slots
        values = tiles_ref[pl.ds(base, slots)].reshape(slots * tile, tile)
        product = jnp.dot(values, rows_ref[j], preferred_element_type=F32)
        count = counts_ref[0, 0, j]
        for s in range(slots):
            place = place_of(pos_ref[0, 0, base + s], mine, z_count)
            place = jnp.where(s < count, place, 2 * half)
            acc_ref[place] += product[s * tile : (s + 1) * tile]
        return carry

    lax.fori_loop(0, blocks, block_step, 0)
    keep_ref[...] = acc_ref[0:half]
    send_ref[...] = acc_ref[half : 2 * half].astype(BF16)


def dense_kernel(parts_ref, weight_ref, bias_ref, grad_ref, act_ref, out_ref):
    tile = grad_ref.shape[0]
    total = parts_ref[0].astype(F32)
    for z in range(1, parts_ref.shape[0]):
        total += parts_ref[z].astype(F32)
    aggregate = total.astype(BF16)
    pre = jnp.dot(aggregate, weight_ref[...], preferred_element_type=F32) + bias_ref[...]
    low = jnp.exp(jnp.minimum(pre, 0.0))
    act_ref[...] = jnp.where(pre > 0, pre, low - 1.0).astype(BF16)
    slope = jnp.where(pre > 0, 1.0, low)
    grad_pre = (grad_ref[...].astype(F32) * slope).astype(BF16)
    out_ref[0:tile] = lax.dot_general(
        weight_ref[...], grad_pre, (((1,), (1,)), ((), ())), preferred_element_type=F32
    ).astype(BF16)
    out_ref[tile:] = lax.dot_general(
        aggregate, grad_pre, (((0,), (0,)), ((), ())), preferred_element_type=F32
    ).astype(BF16)


def backward_kernel(
    z_count, slots, mine_ref, pos_ref, counts_ref, tiles_ref, a_ref, b_ref, c_ref, d_ref, out_ref, held_ref
):
    blocks = out_ref.shape[0]
    tile = tiles_ref.shape[1]
    weight = jnp.zeros((tile, tile), F32)
    for n, ref in enumerate((a_ref, b_ref, c_ref, d_ref)):
        held_ref[n * z_count : (n + 1) * z_count] = ref[0:z_count]
        weight += ref[z_count].astype(F32)
    weight = weight.astype(BF16)
    held_ref[4 * z_count] = jnp.zeros((tile, tile), BF16)
    mine = mine_ref[0]

    def block_step(j, carry):
        base = j * slots
        count = counts_ref[0, 0, j]
        picked = []
        for s in range(slots):
            place = place_of(pos_ref[0, 0, base + s], mine, z_count)
            place = jnp.where(s < count, place, 4 * z_count)
            picked.append(held_ref[place])
        left = jnp.concatenate(picked, axis=1)
        values = tiles_ref[pl.ds(base, slots)].reshape(slots * tile, tile)
        out_ref[j, 0:tile] = jnp.dot(left, values, preferred_element_type=F32).astype(BF16)
        out_ref[j, tile:] = weight
        return carry

    lax.fori_loop(0, blocks, block_step, 0)


def finish_kernel(scale, parts_ref, grad_ref, weight_ref):
    tile = grad_ref.shape[0]
    total = parts_ref[0].astype(F32)
    for n in range(1, parts_ref.shape[0]):
        total += parts_ref[n].astype(F32)
    grad_ref[...] = total[0:tile].T.astype(BF16)
    weight_ref[...] = total[tile:] * scale


def shards(features, weight, bias, tile_vals, tile_pos, tile_counts, grad_out):
    z_count = lax.axis_size("z")
    blocks = lax.axis_size(BLK)
    tile, width = features.shape
    tiles = tile_vals.reshape(tile_vals.shape[2:])
    slots = tiles.shape[0] // blocks
    nodes = tile * lax.axis_size(AXES)
    mine = (lax.axis_index("x_lo") * 2 + lax.axis_index("core")).astype(jnp.int32).reshape(1)
    params = pltpu.CompilerParams(vmem_limit_bytes=LIMIT)
    swap = [(0, 1), (1, 0)]

    rows = lax.all_to_all(jnp.broadcast_to(features[None], (blocks, tile, width)), BLK, 0, 0, tiled=True)
    send, keep = pl.pallas_call(
        functools.partial(forward_kernel, z_count, slots),
        out_shape=(
            jax.ShapeDtypeStruct((2 * z_count, tile, width), BF16),
            jax.ShapeDtypeStruct((2 * z_count, tile, width), F32),
        ),
        in_specs=[SMEM, SMEM, SMEM, VMEM, VMEM],
        out_specs=(VMEM, VMEM),
        scratch_shapes=[pltpu.VMEM((4 * z_count + 1, tile, width), F32)],
        compiler_params=params,
        name="forward",
    )(mine, tile_pos, tile_counts, tiles, rows)
    got = lax.ppermute(send, "core", swap)
    send = (keep[z_count:] + got[z_count:].astype(F32)).astype(BF16)
    keep = keep[:z_count] + got[:z_count].astype(F32)
    got = lax.ppermute(send, "x_lo", swap)
    parts = lax.all_to_all((keep + got.astype(F32)).astype(BF16), "z", 0, 0, tiled=True)

    activations, packed = pl.pallas_call(
        dense_kernel,
        out_shape=(
            jax.ShapeDtypeStruct((tile, width), BF16),
            jax.ShapeDtypeStruct((2 * tile, width), BF16),
        ),
        in_specs=[VMEM] * 4,
        out_specs=(VMEM, VMEM),
        compiler_params=params,
        name="dense",
    )(parts, weight, bias.reshape(1, -1), grad_out)

    gathered = lax.all_gather(packed, "z", axis=0)
    held = jnp.concatenate(
        [gathered[:, :tile], gathered[:, tile:].astype(F32).sum(0, keepdims=True).astype(BF16)], axis=0
    )
    held_x = lax.ppermute(held, "x_lo", swap)
    held_c = lax.ppermute(held, "core", swap)
    held_xc = lax.ppermute(held_x, "core", swap)
    chunks = pl.pallas_call(
        functools.partial(backward_kernel, z_count, slots),
        out_shape=jax.ShapeDtypeStruct((blocks, 2 * tile, width), BF16),
        in_specs=[SMEM, SMEM, SMEM] + [VMEM] * 5,
        out_specs=VMEM,
        scratch_shapes=[pltpu.VMEM((4 * z_count + 1, tile, width), BF16)],
        compiler_params=params,
        name="backward",
    )(mine, tile_pos, tile_counts, tiles, held, held_x, held_c, held_xc)
    parts = lax.all_to_all(chunks, BLK, 0, 0, tiled=True)
    grad_features, grad_weight = pl.pallas_call(
        functools.partial(finish_kernel, 1.0 / math.sqrt(nodes)),
        out_shape=(
            jax.ShapeDtypeStruct((tile, width), BF16),
            jax.ShapeDtypeStruct((width, width), F32),
        ),
        in_specs=[VMEM],
        out_specs=(VMEM, VMEM),
        compiler_params=params,
        name="finish",
    )(parts)
    return (activations, grad_weight, grad_features)


def solution(mesh):
    reps, blks = mesh.devices.shape
    fine = Mesh(mesh.devices.reshape(reps // 4, 2, 2, blks // 2, 2), AXES)
    in_specs = (
        P(AXES, None),
        P(),
        P(),
        P(REP, BLK, None, None, None),
        P(REP, BLK, None),
        P(REP, BLK, None),
        P(AXES, None),
    )
    out_specs = (P(AXES, None), P(), P(AXES, None))
    return jax.shard_map(shards, mesh=fine, in_specs=in_specs, out_specs=out_specs, check_vma=False)
```

```python
import functools
import math

import jax
import jax.numpy as jnp
from jax import lax
from jax.experimental import pallas as pl
from jax.experimental.pallas import tpu as pltpu
from jax.sharding import Mesh, PartitionSpec as P

AXES = ("z", "x_lo", "core", "y", "x_hi")
REP = ("z", "x_lo", "core")
BLK = ("y", "x_hi")
BF16 = jnp.bfloat16
F32 = jnp.float32
VMEM = pl.BlockSpec(memory_space=pltpu.VMEM)
SMEM = pl.BlockSpec(memory_space=pltpu.SMEM)
LIMIT = 24 * 1024 * 1024
FORWARD_LIMIT = 50 * 1024 * 1024
GROUP = 4


def place_of(pos, mine, z_count):
    differs = pos ^ mine
    return ((differs & 1) * 2 + ((differs >> 1) & 1)) * z_count + (pos >> 2)


def forward_kernel(z_count, slots, mine_ref, pos_ref, counts_ref, tiles_ref, rows_ref, send_ref, keep_ref, acc_ref, held_ref, sems):
    blocks, tile, width = rows_ref.shape
    half = 2 * z_count
    mine = mine_ref[0]

    def fetch(j):
        part = pl.ds(j * slots, slots)
        return pltpu.make_async_copy(tiles_ref.at[part], held_ref.at[part], sems.at[j])

    def start_step(j, carry):
        fetch(j).start()
        return carry

    lax.fori_loop(0, blocks, start_step, 0)
    acc_ref[...] = jnp.zeros_like(acc_ref)

    def block_step(j):
        values = held_ref[pl.ds(j * slots, slots)].reshape(slots * tile, tile)
        product = jnp.dot(values, rows_ref[j], preferred_element_type=F32)
        count = counts_ref[0, 0, j]
        for s in range(slots):
            place = place_of(pos_ref[0, 0, j * slots + s], mine, z_count)
            place = jnp.where(s < count, place, 2 * half)
            acc_ref[place] += product[s * tile : (s + 1) * tile]

    def group_step(n, carry):
        for k in range(GROUP):
            fetch(n * GROUP + k).wait()
        for k in range(GROUP):
            block_step(n * GROUP + k)
        return carry

    lax.fori_loop(0, blocks // GROUP, group_step, 0)
    keep_ref[...] = acc_ref[0:half]
    send_ref[...] = acc_ref[half : 2 * half].astype(BF16)


def dense_kernel(parts_ref, weight_ref, bias_ref, grad_ref, act_ref, out_ref):
    tile = grad_ref.shape[0]
    total = parts_ref[0].astype(F32)
    for z in range(1, parts_ref.shape[0]):
        total += parts_ref[z].astype(F32)
    aggregate = total.astype(BF16)
    pre = jnp.dot(aggregate, weight_ref[...], preferred_element_type=F32) + bias_ref[...]
    low = jnp.exp(jnp.minimum(pre, 0.0))
    act_ref[...] = jnp.where(pre > 0, pre, low - 1.0).astype(BF16)
    slope = jnp.where(pre > 0, 1.0, low)
    grad_pre = (grad_ref[...].astype(F32) * slope).astype(BF16)
    out_ref[0:tile] = lax.dot_general(
        weight_ref[...], grad_pre, (((1,), (1,)), ((), ())), preferred_element_type=F32
    ).astype(BF16)
    out_ref[tile:] = lax.dot_general(
        aggregate, grad_pre, (((0,), (0,)), ((), ())), preferred_element_type=F32
    ).astype(BF16)


def column_block(slots, j, mine, pos_ref, counts_ref, tiles_ref, held_ref):
    count_of_places, tile, _ = held_ref.shape
    base = j * slots
    count = counts_ref[0, 0, j]
    picked = []
    for s in range(slots):
        place = place_of(pos_ref[0, 0, base + s], mine, count_of_places // 4)
        picked.append(held_ref[jnp.where(s < count, place, count_of_places - 1)])
    left = jnp.concatenate(picked, axis=1)
    values = tiles_ref[pl.ds(base, slots)].reshape(slots * tile, tile)
    return jnp.dot(left, values, preferred_element_type=F32)


def backward_kernel(
    slots, mine_ref, core_ref, pos_ref, counts_ref, tiles_ref, a_ref, b_ref, c_ref, d_ref, out_ref, held_ref
):
    blocks = out_ref.shape[0]
    tile = tiles_ref.shape[1]
    z_count = a_ref.shape[0] - 1
    for n, ref in enumerate((a_ref, b_ref, c_ref, d_ref)):
        held_ref[n * z_count : (n + 1) * z_count] = ref[0:z_count]
    held_ref[4 * z_count] = jnp.zeros((tile, tile), BF16)
    near = a_ref[z_count].astype(F32) + b_ref[z_count].astype(F32)
    far = c_ref[z_count].astype(F32) + d_ref[z_count].astype(F32)
    total = near + far
    weight = jnp.where(core_ref[0] == 0, total[: tile // 2], total[tile // 2 :]).astype(BF16)

    def block_step(j, carry):
        out = column_block(slots, j, mine_ref[0], pos_ref, counts_ref, tiles_ref, held_ref)
        out_ref[j, 0:tile] = out.astype(BF16)
        out_ref[j, tile:] = weight
        return carry

    lax.fori_loop(0, blocks, block_step, 0, unroll=True)


def finish_kernel(scale, parts_ref, grad_ref, weight_ref):
    tile = grad_ref.shape[0]
    total = parts_ref[0].astype(F32)
    for n in range(1, parts_ref.shape[0]):
        total += parts_ref[n].astype(F32)
    weight_ref[...] = total[tile:] * scale
    grad_ref[...] = total[0:tile].T.astype(BF16)


def shards(features, weight, bias, tile_vals, tile_pos, tile_counts, grad_out):
    z_count = lax.axis_size("z")
    blocks = lax.axis_size(BLK)
    tile, width = features.shape
    tiles = tile_vals.reshape(tile_vals.shape[2:])
    slots = tiles.shape[0] // blocks
    nodes = tile * lax.axis_size(AXES)
    mine = (lax.axis_index("x_lo") * 2 + lax.axis_index("core")).astype(jnp.int32).reshape(1)
    params = pltpu.CompilerParams(vmem_limit_bytes=LIMIT)
    swap = [(0, 1), (1, 0)]
    core = lax.axis_index("core").astype(jnp.int32).reshape(1)
    features, mine, core = lax.optimization_barrier((features, mine, core))

    rows = lax.all_to_all(jnp.broadcast_to(features[None], (blocks, tile, width)), BLK, 0, 0, tiled=True)
    send, keep = pl.pallas_call(
        functools.partial(forward_kernel, z_count, slots),
        out_shape=(
            jax.ShapeDtypeStruct((2 * z_count, tile, width), BF16),
            jax.ShapeDtypeStruct((2 * z_count, tile, width), F32),
        ),
        in_specs=[SMEM, SMEM, SMEM, pl.BlockSpec(memory_space=pl.ANY), VMEM],
        out_specs=(VMEM, VMEM),
        scratch_shapes=[
            pltpu.VMEM((4 * z_count + 1, tile, width), F32),
            pltpu.VMEM(tiles.shape, BF16),
            pltpu.SemaphoreType.DMA((blocks,)),
        ],
        compiler_params=pltpu.CompilerParams(vmem_limit_bytes=FORWARD_LIMIT),
        name="forward",
    )(mine, tile_pos, tile_counts, tiles, rows)
    got = lax.ppermute(send, "core", swap)
    send = (keep[z_count:] + got[z_count:].astype(F32)).astype(BF16)
    keep = keep[:z_count] + got[:z_count].astype(F32)
    got = lax.ppermute(send, "x_lo", swap)
    parts = lax.all_to_all((keep + got.astype(F32)).astype(BF16), "z", 0, 0, tiled=True)

    activations, packed = pl.pallas_call(
        dense_kernel,
        out_shape=(
            jax.ShapeDtypeStruct((tile, width), BF16),
            jax.ShapeDtypeStruct((2 * tile, width), BF16),
        ),
        in_specs=[VMEM] * 4,
        out_specs=(VMEM, VMEM),
        compiler_params=params,
        name="dense",
    )(parts, weight, bias.reshape(1, -1), grad_out)

    gathered = lax.all_gather(packed, "z", axis=0)
    held = jnp.concatenate(
        [gathered[:, :tile], gathered[:, tile:].astype(F32).sum(0, keepdims=True).astype(BF16)], axis=0
    )
    held_x = lax.ppermute(held, "x_lo", swap)
    held_c = lax.ppermute(held, "core", swap)
    held_xc = lax.ppermute(held_x, "core", swap)
    chunks = pl.pallas_call(
        functools.partial(backward_kernel, slots),
        out_shape=jax.ShapeDtypeStruct((blocks, tile + width // 2, width), BF16),
        in_specs=[SMEM] * 4 + [VMEM] * 5,
        out_specs=VMEM,
        scratch_shapes=[pltpu.VMEM((4 * z_count + 1, tile, width), BF16)],
        compiler_params=params,
        name="backward",
    )(mine, core, tile_pos, tile_counts, tiles, held, held_x, held_c, held_xc)
    parts = lax.all_to_all(chunks, BLK, 0, 0, tiled=True)
    grad_features, local = pl.pallas_call(
        functools.partial(finish_kernel, 1.0 / math.sqrt(nodes)),
        out_shape=(
            jax.ShapeDtypeStruct((tile, width), BF16),
            jax.ShapeDtypeStruct((width // 2, width), F32),
        ),
        in_specs=[VMEM],
        out_specs=(VMEM, VMEM),
        compiler_params=params,
        name="finish",
    )(parts)
    other = lax.ppermute(local, "core", swap)
    first = core[0] == 0
    grad_weight = jnp.concatenate([jnp.where(first, local, other), jnp.where(first, other, local)], axis=0)
    return (activations, grad_weight, grad_features)


def solution(mesh):
    reps, blks = mesh.devices.shape
    fine = Mesh(mesh.devices.reshape(reps // 4, 2, 2, blks // 2, 2), AXES)
    in_specs = (
        P(AXES, None),
        P(),
        P(),
        P(REP, BLK, None, None, None),
        P(REP, BLK, None),
        P(REP, BLK, None),
        P(AXES, None),
    )
    out_specs = (P(AXES, None), P(), P(AXES, None))
    return jax.shard_map(shards, mesh=fine, in_specs=in_specs, out_specs=out_specs, check_vma=False)
```

```python
import functools
import math

import jax
import jax.numpy as jnp
from jax import lax
from jax.experimental import pallas as pl
from jax.experimental.pallas import tpu as pltpu
from jax.sharding import Mesh, PartitionSpec as P

AXES = ("z", "x_lo", "core", "y", "x_hi")
REP = ("z", "x_lo", "core")
BLK = ("y", "x_hi")
BF16 = jnp.bfloat16
F32 = jnp.float32
VMEM = pl.BlockSpec(memory_space=pltpu.VMEM)
SMEM = pl.BlockSpec(memory_space=pltpu.SMEM)
LIMIT = 24 * 1024 * 1024
FORWARD_LIMIT = 50 * 1024 * 1024
GROUP = 4


def place_of(pos, mine, z_count):
    differs = pos ^ mine
    return ((differs & 1) * 2 + ((differs >> 1) & 1)) * z_count + (pos >> 2)


def forward_kernel(z_count, slots, mine_ref, pos_ref, counts_ref, tiles_ref, rows_ref, send_ref, keep_ref, acc_ref, held_ref, sems):
    blocks, tile, width = rows_ref.shape
    half = 2 * z_count
    mine = mine_ref[0]

    def fetch(j):
        part = pl.ds(j * slots, slots)
        return pltpu.make_async_copy(tiles_ref.at[part], held_ref.at[part], sems.at[j])

    def start_step(j, carry):
        fetch(j).start()
        return carry

    lax.fori_loop(0, blocks, start_step, 0)
    acc_ref[...] = jnp.zeros_like(acc_ref)

    def block_step(j):
        values = held_ref[pl.ds(j * slots, slots)].reshape(slots * tile, tile)
        product = jnp.dot(values, rows_ref[j], preferred_element_type=F32)
        count = counts_ref[0, 0, j]
        for s in range(slots):
            place = place_of(pos_ref[0, 0, j * slots + s], mine, z_count)
            place = jnp.where(s < count, place, 2 * half)
            acc_ref[place] += product[s * tile : (s + 1) * tile]

    def group_step(n, carry):
        for k in range(GROUP):
            fetch(n * GROUP + k).wait()
        for k in range(GROUP):
            block_step(n * GROUP + k)
        return carry

    lax.fori_loop(0, blocks // GROUP, group_step, 0)
    keep_ref[...] = acc_ref[0:half]
    send_ref[...] = acc_ref[half : 2 * half].astype(BF16)


def dense_kernel(parts_ref, weight_ref, bias_ref, grad_ref, act_ref, out_ref):
    tile = grad_ref.shape[0]
    total = parts_ref[0].astype(F32)
    for z in range(1, parts_ref.shape[0]):
        total += parts_ref[z].astype(F32)
    aggregate = total.astype(BF16)
    pre = jnp.dot(aggregate, weight_ref[...], preferred_element_type=F32) + bias_ref[...]
    low = jnp.exp(jnp.minimum(pre, 0.0))
    act_ref[...] = jnp.where(pre > 0, pre, low - 1.0).astype(BF16)
    slope = jnp.where(pre > 0, 1.0, low)
    grad_pre = (grad_ref[...].astype(F32) * slope).astype(BF16)
    out_ref[0:tile] = lax.dot_general(
        weight_ref[...], grad_pre, (((1,), (1,)), ((), ())), preferred_element_type=F32
    ).astype(BF16)
    out_ref[tile:] = lax.dot_general(
        aggregate, grad_pre, (((0,), (0,)), ((), ())), preferred_element_type=F32
    ).astype(BF16)


def column_block(slots, j, mine, pos_ref, counts_ref, tiles_ref, held_ref):
    count_of_places, tile, _ = held_ref.shape
    base = j * slots
    count = counts_ref[0, 0, j]
    picked = []
    for s in range(slots):
        place = place_of(pos_ref[0, 0, base + s], mine, count_of_places // 4)
        picked.append(held_ref[jnp.where(s < count, place, count_of_places - 1)])
    left = jnp.concatenate(picked, axis=1)
    values = tiles_ref[pl.ds(base, slots)].reshape(slots * tile, tile)
    return jnp.dot(left, values, preferred_element_type=F32)


def backward_send_kernel(
    slots, mine_ref, x_ref, pos_ref, counts_ref, tiles_ref, a_ref, b_ref, c_ref, d_ref, send_ref, held_ref
):
    half, tile, _ = send_ref.shape
    half -= 1
    z_count = a_ref.shape[0] - 1
    for n, ref in enumerate((a_ref, b_ref, c_ref, d_ref)):
        held_ref[n * z_count : (n + 1) * z_count] = ref[0:z_count]
    held_ref[4 * z_count] = jnp.zeros((tile, tile), BF16)
    near = a_ref[z_count].astype(F32) + b_ref[z_count].astype(F32)
    far = c_ref[z_count].astype(F32) + d_ref[z_count].astype(F32)
    send_ref[half] = (near + far).astype(BF16)

    def block_step(y, carry):
        out = column_block(slots, y * 2 + 1 - x_ref[0], mine_ref[0], pos_ref, counts_ref, tiles_ref, held_ref)
        send_ref[y] = out.astype(BF16)
        return carry

    lax.fori_loop(0, half, block_step, 0, unroll=True)


def backward_keep_kernel(slots, mine_ref, x_ref, pos_ref, counts_ref, tiles_ref, held_ref, keep_ref):
    def block_step(y, carry):
        keep_ref[y] = column_block(slots, y * 2 + x_ref[0], mine_ref[0], pos_ref, counts_ref, tiles_ref, held_ref)
        return carry

    lax.fori_loop(0, keep_ref.shape[0], block_step, 0, unroll=True)


def pack_kernel(keep_ref, send_ref, got_ref, out_ref):
    half, tile, _ = keep_ref.shape
    weight = (send_ref[half].astype(F32) + got_ref[half].astype(F32)).astype(BF16)
    for y in range(half):
        out_ref[y, 0:tile] = (keep_ref[y] + got_ref[y].astype(F32)).astype(BF16)
        out_ref[y, tile:] = weight


def finish_kernel(scale, parts_ref, grad_ref, weight_ref):
    tile = grad_ref.shape[0]
    total = parts_ref[0].astype(F32)
    for n in range(1, parts_ref.shape[0]):
        total += parts_ref[n].astype(F32)
    grad_ref[...] = total[0:tile].T.astype(BF16)
    weight_ref[...] = total[tile:] * scale


def shards(features, weight, bias, tile_vals, tile_pos, tile_counts, grad_out):
    z_count = lax.axis_size("z")
    blocks = lax.axis_size(BLK)
    tile, width = features.shape
    tiles = tile_vals.reshape(tile_vals.shape[2:])
    slots = tiles.shape[0] // blocks
    nodes = tile * lax.axis_size(AXES)
    mine = (lax.axis_index("x_lo") * 2 + lax.axis_index("core")).astype(jnp.int32).reshape(1)
    params = pltpu.CompilerParams(vmem_limit_bytes=LIMIT)
    swap = [(0, 1), (1, 0)]
    x_hi = lax.axis_index("x_hi").astype(jnp.int32).reshape(1)
    features, mine, x_hi = lax.optimization_barrier((features, mine, x_hi))

    rows = lax.all_to_all(jnp.broadcast_to(features[None], (blocks, tile, width)), BLK, 0, 0, tiled=True)
    send, keep = pl.pallas_call(
        functools.partial(forward_kernel, z_count, slots),
        out_shape=(
            jax.ShapeDtypeStruct((2 * z_count, tile, width), BF16),
            jax.ShapeDtypeStruct((2 * z_count, tile, width), F32),
        ),
        in_specs=[SMEM, SMEM, SMEM, pl.BlockSpec(memory_space=pl.ANY), VMEM],
        out_specs=(VMEM, VMEM),
        scratch_shapes=[
            pltpu.VMEM((4 * z_count + 1, tile, width), F32),
            pltpu.VMEM(tiles.shape, BF16),
            pltpu.SemaphoreType.DMA((blocks,)),
        ],
        compiler_params=pltpu.CompilerParams(vmem_limit_bytes=FORWARD_LIMIT),
        name="forward",
    )(mine, tile_pos, tile_counts, tiles, rows)
    got = lax.ppermute(send, "core", swap)
    send = (keep[z_count:] + got[z_count:].astype(F32)).astype(BF16)
    keep = keep[:z_count] + got[:z_count].astype(F32)
    got = lax.ppermute(send, "x_lo", swap)
    parts = lax.all_to_all((keep + got.astype(F32)).astype(BF16), "z", 0, 0, tiled=True)

    activations, packed = pl.pallas_call(
        dense_kernel,
        out_shape=(
            jax.ShapeDtypeStruct((tile, width), BF16),
            jax.ShapeDtypeStruct((2 * tile, width), BF16),
        ),
        in_specs=[VMEM] * 4,
        out_specs=(VMEM, VMEM),
        compiler_params=params,
        name="dense",
    )(parts, weight, bias.reshape(1, -1), grad_out)

    gathered = lax.all_gather(packed, "z", axis=0)
    held = jnp.concatenate(
        [gathered[:, :tile], gathered[:, tile:].astype(F32).sum(0, keepdims=True).astype(BF16)], axis=0
    )
    held_x = lax.ppermute(held, "x_lo", swap)
    held_c = lax.ppermute(held, "core", swap)
    held_xc = lax.ppermute(held_x, "core", swap)
    half = blocks // 2
    send, places = pl.pallas_call(
        functools.partial(backward_send_kernel, slots),
        out_shape=(
            jax.ShapeDtypeStruct((half + 1, tile, width), BF16),
            jax.ShapeDtypeStruct((4 * z_count + 1, tile, width), BF16),
        ),
        in_specs=[SMEM] * 4 + [VMEM] * 5,
        out_specs=(VMEM, VMEM),
        compiler_params=params,
        name="backward_send",
    )(mine, x_hi, tile_pos, tile_counts, tiles, held, held_x, held_c, held_xc)
    got = lax.ppermute(send, "x_hi", swap)
    keep = pl.pallas_call(
        functools.partial(backward_keep_kernel, slots),
        out_shape=jax.ShapeDtypeStruct((half, tile, width), F32),
        in_specs=[SMEM] * 4 + [VMEM] * 2,
        out_specs=VMEM,
        compiler_params=params,
        cost_estimate=pl.CostEstimate(flops=tiles.size * width, bytes_accessed=tiles.size, transcendentals=0),
        name="backward_keep",
    )(mine, x_hi, tile_pos, tile_counts, tiles, places)
    chunks = pl.pallas_call(
        pack_kernel,
        out_shape=jax.ShapeDtypeStruct((half, 2 * tile, width), BF16),
        in_specs=[VMEM] * 3,
        out_specs=VMEM,
        compiler_params=params,
        name="pack",
    )(keep, send, got)
    parts = lax.all_to_all(chunks, "y", 0, 0, tiled=True)
    grad_features, grad_weight = pl.pallas_call(
        functools.partial(finish_kernel, 1.0 / math.sqrt(nodes)),
        out_shape=(
            jax.ShapeDtypeStruct((tile, width), BF16),
            jax.ShapeDtypeStruct((width, width), F32),
        ),
        in_specs=[VMEM],
        out_specs=(VMEM, VMEM),
        compiler_params=params,
        name="finish",
    )(parts)
    return (activations, grad_weight, grad_features)


def solution(mesh):
    reps, blks = mesh.devices.shape
    fine = Mesh(mesh.devices.reshape(reps // 4, 2, 2, blks // 2, 2), AXES)
    in_specs = (
        P(AXES, None),
        P(),
        P(),
        P(REP, BLK, None, None, None),
        P(REP, BLK, None),
        P(REP, BLK, None),
        P(AXES, None),
    )
    out_specs = (P(AXES, None), P(), P(AXES, None))
    return jax.shard_map(shards, mesh=fine, in_specs=in_specs, out_specs=out_specs, check_vma=False)
```

```python
import functools
import math

import jax
import jax.numpy as jnp
from jax import lax
from jax.experimental import pallas as pl
from jax.experimental.pallas import tpu as pltpu
from jax.sharding import Mesh, PartitionSpec as P

AXES = ("z_hi", "z_lo", "x_lo", "core", "y_hi", "y_lo", "x_hi")
Z = ("z_hi", "z_lo")
REP = ("z_hi", "z_lo", "x_lo", "core")
BLK = ("y_hi", "y_lo", "x_hi")
BF16 = jnp.bfloat16
F32 = jnp.float32
VMEM = pl.BlockSpec(memory_space=pltpu.VMEM)
SMEM = pl.BlockSpec(memory_space=pltpu.SMEM)
LIMIT = 24 * 1024 * 1024
FORWARD_LIMIT = 50 * 1024 * 1024
GROUP = 4


def place_of(pos, mine, z_count):
    differs = pos ^ mine
    return ((differs & 1) * 2 + ((differs >> 1) & 1)) * z_count + (pos >> 2)


def chunk_of(pos, mine, z_count):
    return ((pos ^ mine) & 1) * (2 * z_count) + ((pos >> 1) & 3) * (z_count // 2) + (pos >> 3)


def forward_kernel(z_count, slots, mine_ref, pos_ref, counts_ref, tiles_ref, rows_ref, send_ref, keep_ref, acc_ref, held_ref, sems):
    blocks, tile, width = rows_ref.shape
    half = 2 * z_count
    mine = mine_ref[0]

    def fetch(j):
        part = pl.ds(j * slots, slots)
        return pltpu.make_async_copy(tiles_ref.at[part], held_ref.at[part], sems.at[j])

    def start_step(j, carry):
        fetch(j).start()
        return carry

    lax.fori_loop(0, blocks, start_step, 0)
    acc_ref[...] = jnp.zeros_like(acc_ref)

    def block_step(j):
        values = held_ref[pl.ds(j * slots, slots)].reshape(slots * tile, tile)
        product = jnp.dot(values, rows_ref[j], preferred_element_type=F32)
        count = counts_ref[0, 0, j]
        for s in range(slots):
            place = chunk_of(pos_ref[0, 0, j * slots + s], mine, z_count)
            place = jnp.where(s < count, place, 2 * half)
            acc_ref[place] += product[s * tile : (s + 1) * tile]

    def group_step(n, carry):
        for k in range(GROUP):
            fetch(n * GROUP + k).wait()
        for k in range(GROUP):
            block_step(n * GROUP + k)
        return carry

    lax.fori_loop(0, blocks // GROUP, group_step, 0)
    keep_ref[...] = acc_ref[0:half]
    send_ref[...] = acc_ref[half : 2 * half].astype(BF16)


def near_sum_kernel(parts_ref, out_ref):
    for z in range(out_ref.shape[0]):
        total = parts_ref[0, z].astype(F32)
        for n in range(1, parts_ref.shape[0]):
            total += parts_ref[n, z].astype(F32)
        out_ref[z] = total.astype(BF16)


def dense_kernel(parts_ref, weight_ref, bias_ref, grad_ref, act_ref, out_ref):
    tile = grad_ref.shape[0]
    total = parts_ref[0].astype(F32)
    for z in range(1, parts_ref.shape[0]):
        total += parts_ref[z].astype(F32)
    aggregate = total.astype(BF16)
    pre = jnp.dot(aggregate, weight_ref[...], preferred_element_type=F32) + bias_ref[...]
    low = jnp.exp(jnp.minimum(pre, 0.0))
    act_ref[...] = jnp.where(pre > 0, pre, low - 1.0).astype(BF16)
    slope = jnp.where(pre > 0, 1.0, low)
    grad_pre = (grad_ref[...].astype(F32) * slope).astype(BF16)
    out_ref[0:tile] = lax.dot_general(
        weight_ref[...], grad_pre, (((1,), (1,)), ((), ())), preferred_element_type=F32
    ).astype(BF16)
    out_ref[tile:] = lax.dot_general(
        aggregate, grad_pre, (((0,), (0,)), ((), ())), preferred_element_type=F32
    ).astype(BF16)


def column_block(slots, j, mine, pos_ref, counts_ref, tiles_ref, held_ref):
    count_of_places, tile, _ = held_ref.shape
    base = j * slots
    count = counts_ref[0, 0, j]
    picked = []
    for s in range(slots):
        place = place_of(pos_ref[0, 0, base + s], mine, count_of_places // 4)
        picked.append(held_ref[jnp.where(s < count, place, count_of_places - 1)])
    left = jnp.concatenate(picked, axis=1)
    values = tiles_ref[pl.ds(base, slots)].reshape(slots * tile, tile)
    return jnp.dot(left, values, preferred_element_type=F32)


def backward_kernel(
    slots, mine_ref, pos_ref, counts_ref, tiles_ref, a_ref, b_ref, c_ref, d_ref, out_ref, held_ref
):
    near_count, far_count, tile, _ = out_ref.shape
    far_count -= 1
    z_count = a_ref.shape[0] - 1
    for n, ref in enumerate((a_ref, b_ref, c_ref, d_ref)):
        held_ref[n * z_count : (n + 1) * z_count] = ref[0:z_count]
    held_ref[4 * z_count] = jnp.zeros((tile, tile), BF16)
    near = a_ref[z_count].astype(F32) + b_ref[z_count].astype(F32)
    far = c_ref[z_count].astype(F32) + d_ref[z_count].astype(F32)
    weight = (near + far).astype(BF16)
    for n in range(near_count):
        for m in range(far_count):
            out = column_block(slots, m * near_count + n, mine_ref[0], pos_ref, counts_ref, tiles_ref, held_ref)
            out_ref[n, m] = out.astype(BF16)
        out_ref[n, far_count] = weight


def pack_kernel(parts_ref, out_ref):
    far_count = out_ref.shape[0]
    tile = parts_ref.shape[2]

    def total(m):
        out = parts_ref[0, m].astype(F32)
        for n in range(1, parts_ref.shape[0]):
            out += parts_ref[n, m].astype(F32)
        return out.astype(BF16)

    weight = total(far_count)
    for m in range(far_count):
        out_ref[m, 0:tile] = total(m)
        out_ref[m, tile:] = weight


def finish_kernel(scale, parts_ref, grad_ref, weight_ref):
    tile = grad_ref.shape[0]
    total = parts_ref[0].astype(F32)
    for n in range(1, parts_ref.shape[0]):
        total += parts_ref[n].astype(F32)
    grad_ref[...] = total[0:tile].T.astype(BF16)
    weight_ref[...] = total[tile:] * scale


def shards(features, weight, bias, tile_vals, tile_pos, tile_counts, grad_out):
    z_count = lax.axis_size(Z)
    blocks = lax.axis_size(BLK)
    tile, width = features.shape
    tiles = tile_vals.reshape(tile_vals.shape[2:])
    slots = tiles.shape[0] // blocks
    nodes = tile * lax.axis_size(AXES)
    mine = (lax.axis_index("x_lo") * 2 + lax.axis_index("core")).astype(jnp.int32).reshape(1)
    params = pltpu.CompilerParams(vmem_limit_bytes=LIMIT)
    swap = [(0, 1), (1, 0)]
    features, mine = lax.optimization_barrier((features, mine))

    rows = lax.all_to_all(jnp.broadcast_to(features[None], (blocks, tile, width)), BLK, 0, 0, tiled=True)
    send, keep = pl.pallas_call(
        functools.partial(forward_kernel, z_count, slots),
        out_shape=(
            jax.ShapeDtypeStruct((2 * z_count, tile, width), BF16),
            jax.ShapeDtypeStruct((2 * z_count, tile, width), F32),
        ),
        in_specs=[SMEM, SMEM, SMEM, pl.BlockSpec(memory_space=pl.ANY), VMEM],
        out_specs=(VMEM, VMEM),
        scratch_shapes=[
            pltpu.VMEM((4 * z_count + 1, tile, width), F32),
            pltpu.VMEM(tiles.shape, BF16),
            pltpu.SemaphoreType.DMA((blocks,)),
        ],
        compiler_params=pltpu.CompilerParams(vmem_limit_bytes=FORWARD_LIMIT),
        name="forward",
    )(mine, tile_pos, tile_counts, tiles, rows)
    got = lax.ppermute(send, "core", swap)
    parts = (keep + got.astype(F32)).astype(BF16).reshape(4, z_count // 2, tile, width)
    parts = lax.all_to_all(parts, ("z_lo", "x_lo"), 0, 0, tiled=True)
    parts = pl.pallas_call(
        near_sum_kernel,
        out_shape=jax.ShapeDtypeStruct(parts.shape[1:], BF16),
        in_specs=[VMEM],
        out_specs=VMEM,
        compiler_params=params,
        name="near_sum",
    )(parts)
    parts = lax.all_to_all(parts, "z_hi", 0, 0, tiled=True)

    activations, packed = pl.pallas_call(
        dense_kernel,
        out_shape=(
            jax.ShapeDtypeStruct((tile, width), BF16),
            jax.ShapeDtypeStruct((2 * tile, width), BF16),
        ),
        in_specs=[VMEM] * 4,
        out_specs=(VMEM, VMEM),
        compiler_params=params,
        name="dense",
    )(parts, weight, bias.reshape(1, -1), grad_out)

    gathered = lax.all_gather(packed, Z, axis=0)
    held = jnp.concatenate(
        [gathered[:, :tile], gathered[:, tile:].astype(F32).sum(0, keepdims=True).astype(BF16)], axis=0
    )
    held_x = lax.ppermute(held, "x_lo", swap)
    held_c = lax.ppermute(held, "core", swap)
    held_xc = lax.ppermute(held_x, "core", swap)
    near_count = lax.axis_size(("y_lo", "x_hi"))
    far_count = blocks // near_count
    chunks = pl.pallas_call(
        functools.partial(backward_kernel, slots),
        out_shape=jax.ShapeDtypeStruct((near_count, far_count + 1, tile, width), BF16),
        in_specs=[SMEM] * 3 + [VMEM] * 5,
        out_specs=VMEM,
        scratch_shapes=[pltpu.VMEM((4 * z_count + 1, tile, width), BF16)],
        compiler_params=params,
        name="backward",
    )(mine, tile_pos, tile_counts, tiles, held, held_x, held_c, held_xc)
    parts = lax.all_to_all(chunks, ("y_lo", "x_hi"), 0, 0, tiled=True)
    chunks = pl.pallas_call(
        pack_kernel,
        out_shape=jax.ShapeDtypeStruct((far_count, 2 * tile, width), BF16),
        in_specs=[VMEM],
        out_specs=VMEM,
        compiler_params=params,
        name="pack",
    )(parts)
    parts = lax.all_to_all(chunks, "y_hi", 0, 0, tiled=True)
    grad_features, grad_weight = pl.pallas_call(
        functools.partial(finish_kernel, 1.0 / math.sqrt(nodes)),
        out_shape=(
            jax.ShapeDtypeStruct((tile, width), BF16),
            jax.ShapeDtypeStruct((width, width), F32),
        ),
        in_specs=[VMEM],
        out_specs=(VMEM, VMEM),
        compiler_params=params,
        name="finish",
    )(parts)
    return (activations, grad_weight, grad_features)


def solution(mesh):
    reps, blks = mesh.devices.shape
    fine = Mesh(mesh.devices.reshape(reps // 8, 2, 2, 2, blks // 4, 2, 2), AXES)
    in_specs = (
        P(AXES, None),
        P(),
        P(),
        P(REP, BLK, None, None, None),
        P(REP, BLK, None),
        P(REP, BLK, None),
        P(AXES, None),
    )
    out_specs = (P(AXES, None), P(), P(AXES, None))
    return jax.shard_map(shards, mesh=fine, in_specs=in_specs, out_specs=out_specs, check_vma=False)
```

```python
import functools
import math

import jax
import jax.numpy as jnp
from jax import lax
from jax.experimental import pallas as pl
from jax.experimental.pallas import tpu as pltpu
from jax.sharding import Mesh, PartitionSpec as P

AXES = ("z_hi", "z_lo", "x_lo", "core", "y_hi", "y_lo", "x_hi")
Z = ("z_hi", "z_lo")
REP = ("z_hi", "z_lo", "x_lo", "core")
BLK = ("y_hi", "y_lo", "x_hi")
BF16 = jnp.bfloat16
F32 = jnp.float32
VMEM = pl.BlockSpec(memory_space=pltpu.VMEM)
SMEM = pl.BlockSpec(memory_space=pltpu.SMEM)
LIMIT = 24 * 1024 * 1024
FORWARD_LIMIT = 50 * 1024 * 1024
GROUP = 4


def chunk_of(pos, mine, z_count):
    return ((pos ^ mine) & 1) * (2 * z_count) + ((pos >> 1) & 3) * (z_count // 2) + (pos >> 3)


def forward_kernel(z_count, slots, mine_ref, pos_ref, counts_ref, tiles_ref, rows_ref, send_ref, keep_ref, acc_ref, held_ref, sems):
    blocks, tile, width = rows_ref.shape
    half = 2 * z_count
    mine = mine_ref[0]

    def fetch(j):
        part = pl.ds(j * slots, slots)
        return pltpu.make_async_copy(tiles_ref.at[part], held_ref.at[part], sems.at[j])

    def start_step(j, carry):
        fetch(j).start()
        return carry

    lax.fori_loop(0, blocks, start_step, 0)
    acc_ref[...] = jnp.zeros_like(acc_ref)

    def block_step(j):
        values = held_ref[pl.ds(j * slots, slots)].reshape(slots * tile, tile)
        product = jnp.dot(values, rows_ref[j], preferred_element_type=F32)
        count = counts_ref[0, 0, j]
        for s in range(slots):
            place = chunk_of(pos_ref[0, 0, j * slots + s], mine, z_count)
            place = jnp.where(s < count, place, 2 * half)
            acc_ref[place] += product[s * tile : (s + 1) * tile]

    def group_step(n, carry):
        for k in range(GROUP):
            fetch(n * GROUP + k).wait()
        for k in range(GROUP):
            block_step(n * GROUP + k)
        return carry

    lax.fori_loop(0, blocks // GROUP, group_step, 0)
    keep_ref[...] = acc_ref[0:half]
    send_ref[...] = acc_ref[half : 2 * half].astype(BF16)


def near_sum_kernel(parts_ref, out_ref):
    for z in range(out_ref.shape[0]):
        total = parts_ref[0, z].astype(F32)
        for n in range(1, parts_ref.shape[0]):
            total += parts_ref[n, z].astype(F32)
        out_ref[z] = total.astype(BF16)


def dense_kernel(parts_ref, weight_ref, bias_ref, grad_ref, act_ref, out_ref):
    tile = grad_ref.shape[0]
    total = parts_ref[0].astype(F32)
    for z in range(1, parts_ref.shape[0]):
        total += parts_ref[z].astype(F32)
    aggregate = total.astype(BF16)
    pre = jnp.dot(aggregate, weight_ref[...], preferred_element_type=F32) + bias_ref[...]
    low = jnp.exp(jnp.minimum(pre, 0.0))
    act_ref[...] = jnp.where(pre > 0, pre, low - 1.0).astype(BF16)
    slope = jnp.where(pre > 0, 1.0, low)
    grad_pre = (grad_ref[...].astype(F32) * slope).astype(BF16)
    out_ref[0:tile] = lax.dot_general(
        weight_ref[...], grad_pre, (((1,), (1,)), ((), ())), preferred_element_type=F32
    ).astype(BF16)
    out_ref[tile:] = lax.dot_general(
        aggregate, grad_pre, (((0,), (0,)), ((), ())), preferred_element_type=F32
    ).astype(BF16)


def column_block(slots, j, mine, pos_ref, counts_ref, tiles_ref, held_ref):
    count_of_places, tile, _ = held_ref.shape
    base = j * slots
    count = counts_ref[0, 0, j]
    picked = []
    for s in range(slots):
        place = chunk_of(pos_ref[0, 0, base + s], mine, count_of_places // 4)
        picked.append(held_ref[jnp.where(s < count, place, count_of_places - 1)])
    left = jnp.concatenate(picked, axis=1)
    values = tiles_ref[pl.ds(base, slots)].reshape(slots * tile, tile)
    return jnp.dot(left, values, preferred_element_type=F32)


def backward_kernel(
    slots, mine_ref, pos_ref, counts_ref, tiles_ref, own_ref, other_ref, out_ref, held_ref
):
    near_count, far_count, tile, _ = out_ref.shape
    far_count -= 1
    groups, each = own_ref.shape[0], own_ref.shape[1] - 1
    sums = []
    for n, ref in enumerate((own_ref, other_ref)):
        part = jnp.zeros((tile, tile), F32)
        for g in range(groups):
            held_ref[pl.ds((n * groups + g) * each, each)] = ref[g, 0:each]
            part += ref[g, each].astype(F32)
        sums.append(part)
    held_ref[2 * groups * each] = jnp.zeros((tile, tile), BF16)
    near, far = sums
    weight = (near + far).astype(BF16)
    for n in range(near_count):
        for m in range(far_count):
            out = column_block(slots, m * near_count + n, mine_ref[0], pos_ref, counts_ref, tiles_ref, held_ref)
            out_ref[n, m] = out.astype(BF16)
        out_ref[n, far_count] = weight


def pack_kernel(parts_ref, out_ref):
    far_count = out_ref.shape[0]
    tile = parts_ref.shape[2]

    def total(m):
        out = parts_ref[0, m].astype(F32)
        for n in range(1, parts_ref.shape[0]):
            out += parts_ref[n, m].astype(F32)
        return out.astype(BF16)

    weight = total(far_count)
    for m in range(far_count):
        out_ref[m, 0:tile] = total(m)
        out_ref[m, tile:] = weight


def finish_kernel(scale, parts_ref, grad_ref, weight_ref):
    tile = grad_ref.shape[0]
    total = parts_ref[0].astype(F32)
    for n in range(1, parts_ref.shape[0]):
        total += parts_ref[n].astype(F32)
    grad_ref[...] = total[0:tile].T.astype(BF16)
    weight_ref[...] = total[tile:] * scale


def shards(features, weight, bias, tile_vals, tile_pos, tile_counts, grad_out):
    z_count = lax.axis_size(Z)
    blocks = lax.axis_size(BLK)
    tile, width = features.shape
    tiles = tile_vals.reshape(tile_vals.shape[2:])
    slots = tiles.shape[0] // blocks
    nodes = tile * lax.axis_size(AXES)
    mine = (lax.axis_index("x_lo") * 2 + lax.axis_index("core")).astype(jnp.int32).reshape(1)
    params = pltpu.CompilerParams(vmem_limit_bytes=LIMIT)
    swap = [(0, 1), (1, 0)]
    features, mine = lax.optimization_barrier((features, mine))

    rows = lax.all_to_all(jnp.broadcast_to(features[None], (blocks, tile, width)), BLK, 0, 0, tiled=True)
    send, keep = pl.pallas_call(
        functools.partial(forward_kernel, z_count, slots),
        out_shape=(
            jax.ShapeDtypeStruct((2 * z_count, tile, width), BF16),
            jax.ShapeDtypeStruct((2 * z_count, tile, width), F32),
        ),
        in_specs=[SMEM, SMEM, SMEM, pl.BlockSpec(memory_space=pl.ANY), VMEM],
        out_specs=(VMEM, VMEM),
        scratch_shapes=[
            pltpu.VMEM((4 * z_count + 1, tile, width), F32),
            pltpu.VMEM(tiles.shape, BF16),
            pltpu.SemaphoreType.DMA((blocks,)),
        ],
        compiler_params=pltpu.CompilerParams(vmem_limit_bytes=FORWARD_LIMIT),
        name="forward",
    )(mine, tile_pos, tile_counts, tiles, rows)
    got = lax.ppermute(send, "core", swap)
    parts = (keep + got.astype(F32)).astype(BF16).reshape(4, z_count // 2, tile, width)
    parts = lax.all_to_all(parts, ("z_lo", "x_lo"), 0, 0, tiled=True)
    parts = pl.pallas_call(
        near_sum_kernel,
        out_shape=jax.ShapeDtypeStruct(parts.shape[1:], BF16),
        in_specs=[VMEM],
        out_specs=VMEM,
        compiler_params=params,
        name="near_sum",
    )(parts)
    parts = lax.all_to_all(parts, "z_hi", 0, 0, tiled=True)

    activations, packed = pl.pallas_call(
        dense_kernel,
        out_shape=(
            jax.ShapeDtypeStruct((tile, width), BF16),
            jax.ShapeDtypeStruct((2 * tile, width), BF16),
        ),
        in_specs=[VMEM] * 4,
        out_specs=(VMEM, VMEM),
        compiler_params=params,
        name="dense",
    )(parts, weight, bias.reshape(1, -1), grad_out)

    gathered = lax.all_gather(packed, "z_hi", axis=0)
    held = jnp.concatenate(
        [gathered[:, :tile], gathered[:, tile:].astype(F32).sum(0, keepdims=True).astype(BF16)], axis=0
    )
    own = lax.all_to_all(jnp.broadcast_to(held[None], (4, *held.shape)), ("z_lo", "x_lo"), 0, 0, tiled=True)
    other = lax.ppermute(own, "core", swap)
    near_count = lax.axis_size(("y_lo", "x_hi"))
    far_count = blocks // near_count
    chunks = pl.pallas_call(
        functools.partial(backward_kernel, slots),
        out_shape=jax.ShapeDtypeStruct((near_count, far_count + 1, tile, width), BF16),
        in_specs=[SMEM] * 3 + [VMEM] * 3,
        out_specs=VMEM,
        scratch_shapes=[pltpu.VMEM((4 * z_count + 1, tile, width), BF16)],
        compiler_params=params,
        name="backward",
    )(mine, tile_pos, tile_counts, tiles, own, other)
    parts = lax.all_to_all(chunks, ("y_lo", "x_hi"), 0, 0, tiled=True)
    chunks = pl.pallas_call(
        pack_kernel,
        out_shape=jax.ShapeDtypeStruct((far_count, 2 * tile, width), BF16),
        in_specs=[VMEM],
        out_specs=VMEM,
        compiler_params=params,
        name="pack",
    )(parts)
    parts = lax.all_to_all(chunks, "y_hi", 0, 0, tiled=True)
    grad_features, grad_weight = pl.pallas_call(
        functools.partial(finish_kernel, 1.0 / math.sqrt(nodes)),
        out_shape=(
            jax.ShapeDtypeStruct((tile, width), BF16),
            jax.ShapeDtypeStruct((width, width), F32),
        ),
        in_specs=[VMEM],
        out_specs=(VMEM, VMEM),
        compiler_params=params,
        name="finish",
    )(parts)
    return (activations, grad_weight, grad_features)


def solution(mesh):
    reps, blks = mesh.devices.shape
    fine = Mesh(mesh.devices.reshape(reps // 8, 2, 2, 2, blks // 4, 2, 2), AXES)
    in_specs = (
        P(AXES, None),
        P(),
        P(),
        P(REP, BLK, None, None, None),
        P(REP, BLK, None),
        P(REP, BLK, None),
        P(AXES, None),
    )
    out_specs = (P(AXES, None), P(), P(AXES, None))
    return jax.shard_map(shards, mesh=fine, in_specs=in_specs, out_specs=out_specs, check_vma=False)
```

```python
import functools
import math

import jax
import jax.numpy as jnp
from jax import lax
from jax.experimental import pallas as pl
from jax.experimental.pallas import tpu as pltpu
from jax.sharding import Mesh, PartitionSpec as P

AXES = ("z_hi", "z_lo", "x_lo", "core", "y_hi", "y_lo", "x_hi")
Z = ("z_hi", "z_lo")
REP = ("z_hi", "z_lo", "x_lo", "core")
BLK = ("y_hi", "y_lo", "x_hi")
BF16 = jnp.bfloat16
F32 = jnp.float32
VMEM = pl.BlockSpec(memory_space=pltpu.VMEM)
SMEM = pl.BlockSpec(memory_space=pltpu.SMEM)
LIMIT = 24 * 1024 * 1024
FORWARD_LIMIT = 50 * 1024 * 1024
GROUP = 4


def chunk_of(pos, mine, z_count):
    return ((pos ^ mine) & 1) * (2 * z_count) + ((pos >> 1) & 3) * (z_count // 2) + (pos >> 3)


def forward_kernel(z_count, slots, mine_ref, pos_ref, counts_ref, tiles_ref, rows_ref, send_ref, keep_ref, acc_ref, held_ref, sems):
    near_count, far_count, tile, width = rows_ref.shape
    blocks = near_count * far_count
    half = 2 * z_count
    mine = mine_ref[0]

    def fetch(j):
        part = pl.ds(j * slots, slots)
        return pltpu.make_async_copy(tiles_ref.at[part], held_ref.at[part], sems.at[j])

    def start_step(j, carry):
        fetch(j).start()
        return carry

    lax.fori_loop(0, blocks, start_step, 0)
    acc_ref[...] = jnp.zeros_like(acc_ref)

    def block_step(j):
        values = held_ref[pl.ds(j * slots, slots)].reshape(slots * tile, tile)
        product = jnp.dot(values, rows_ref[j % near_count, j // near_count], preferred_element_type=F32)
        count = counts_ref[0, 0, j]
        for s in range(slots):
            place = chunk_of(pos_ref[0, 0, j * slots + s], mine, z_count)
            place = jnp.where(s < count, place, 2 * half)
            acc_ref[place] += product[s * tile : (s + 1) * tile]

    def group_step(n, carry):
        for k in range(GROUP):
            fetch(n * GROUP + k).wait()
        for k in range(GROUP):
            block_step(n * GROUP + k)
        return carry

    lax.fori_loop(0, blocks // GROUP, group_step, 0)
    keep_ref[...] = acc_ref[0:half]
    send_ref[...] = acc_ref[half : 2 * half].astype(BF16)


def near_sum_kernel(parts_ref, out_ref):
    for z in range(out_ref.shape[0]):
        total = parts_ref[0, z].astype(F32)
        for n in range(1, parts_ref.shape[0]):
            total += parts_ref[n, z].astype(F32)
        out_ref[z] = total.astype(BF16)


def dense_kernel(parts_ref, weight_ref, bias_ref, grad_ref, act_ref, out_ref):
    tile = grad_ref.shape[0]
    total = parts_ref[0].astype(F32)
    for z in range(1, parts_ref.shape[0]):
        total += parts_ref[z].astype(F32)
    aggregate = total.astype(BF16)
    pre = jnp.dot(aggregate, weight_ref[...], preferred_element_type=F32) + bias_ref[...]
    low = jnp.exp(jnp.minimum(pre, 0.0))
    act_ref[...] = jnp.where(pre > 0, pre, low - 1.0).astype(BF16)
    slope = jnp.where(pre > 0, 1.0, low)
    grad_pre = (grad_ref[...].astype(F32) * slope).astype(BF16)
    out_ref[0:tile] = lax.dot_general(
        weight_ref[...], grad_pre, (((1,), (1,)), ((), ())), preferred_element_type=F32
    ).astype(BF16)
    out_ref[tile:] = lax.dot_general(
        aggregate, grad_pre, (((0,), (0,)), ((), ())), preferred_element_type=F32
    ).astype(BF16)


def column_block(slots, j, mine, pos_ref, counts_ref, tiles_ref, held_ref):
    count_of_places, tile, _ = held_ref.shape
    base = j * slots
    count = counts_ref[0, 0, j]
    picked = []
    for s in range(slots):
        place = chunk_of(pos_ref[0, 0, base + s], mine, count_of_places // 4)
        picked.append(held_ref[jnp.where(s < count, place, count_of_places - 1)])
    left = jnp.concatenate(picked, axis=1)
    values = tiles_ref[pl.ds(base, slots)].reshape(slots * tile, tile)
    return jnp.dot(left, values, preferred_element_type=F32)


def backward_kernel(
    slots, mine_ref, pos_ref, counts_ref, tiles_ref, own_ref, other_ref, out_ref, held_ref
):
    near_count, far_count, tile, _ = out_ref.shape
    far_count -= 1
    groups, each = own_ref.shape[0], own_ref.shape[1] - 1
    sums = []
    for n, ref in enumerate((own_ref, other_ref)):
        part = jnp.zeros((tile, tile), F32)
        for g in range(groups):
            held_ref[pl.ds((n * groups + g) * each, each)] = ref[g, 0:each]
            part += ref[g, each].astype(F32)
        sums.append(part)
    held_ref[2 * groups * each] = jnp.zeros((tile, tile), BF16)
    near, far = sums
    weight = (near + far).astype(BF16)
    for n in range(near_count):
        for m in range(far_count):
            out = column_block(slots, m * near_count + n, mine_ref[0], pos_ref, counts_ref, tiles_ref, held_ref)
            out_ref[n, m] = out.astype(BF16)
        out_ref[n, far_count] = weight


def pack_kernel(parts_ref, out_ref):
    far_count = out_ref.shape[0]
    tile = parts_ref.shape[2]

    def total(m):
        out = parts_ref[0, m].astype(F32)
        for n in range(1, parts_ref.shape[0]):
            out += parts_ref[n, m].astype(F32)
        return out.astype(BF16)

    weight = total(far_count)
    for m in range(far_count):
        out_ref[m, 0:tile] = total(m)
        out_ref[m, tile:] = weight


def finish_kernel(scale, parts_ref, grad_ref, weight_ref):
    tile = grad_ref.shape[0]
    total = parts_ref[0].astype(F32)
    for n in range(1, parts_ref.shape[0]):
        total += parts_ref[n].astype(F32)
    grad_ref[...] = total[0:tile].T.astype(BF16)
    weight_ref[...] = total[tile:] * scale


def shards(features, weight, bias, tile_vals, tile_pos, tile_counts, grad_out):
    z_count = lax.axis_size(Z)
    blocks = lax.axis_size(BLK)
    tile, width = features.shape
    tiles = tile_vals.reshape(tile_vals.shape[2:])
    slots = tiles.shape[0] // blocks
    nodes = tile * lax.axis_size(AXES)
    mine = (lax.axis_index("x_lo") * 2 + lax.axis_index("core")).astype(jnp.int32).reshape(1)
    params = pltpu.CompilerParams(vmem_limit_bytes=LIMIT)
    swap = [(0, 1), (1, 0)]
    features, mine = lax.optimization_barrier((features, mine))

    near_count = lax.axis_size(("y_lo", "x_hi"))
    far_count = blocks // near_count
    rows = lax.all_to_all(jnp.broadcast_to(features[None], (far_count, tile, width)), "y_hi", 0, 0, tiled=True)
    rows = jnp.broadcast_to(rows[None], (near_count, far_count, tile, width))
    rows = lax.all_to_all(rows, ("y_lo", "x_hi"), 0, 0, tiled=True)
    send, keep = pl.pallas_call(
        functools.partial(forward_kernel, z_count, slots),
        out_shape=(
            jax.ShapeDtypeStruct((2 * z_count, tile, width), BF16),
            jax.ShapeDtypeStruct((2 * z_count, tile, width), F32),
        ),
        in_specs=[SMEM, SMEM, SMEM, pl.BlockSpec(memory_space=pl.ANY), VMEM],
        out_specs=(VMEM, VMEM),
        scratch_shapes=[
            pltpu.VMEM((4 * z_count + 1, tile, width), F32),
            pltpu.VMEM(tiles.shape, BF16),
            pltpu.SemaphoreType.DMA((blocks,)),
        ],
        compiler_params=pltpu.CompilerParams(vmem_limit_bytes=FORWARD_LIMIT),
        name="forward",
    )(mine, tile_pos, tile_counts, tiles, rows)
    got = lax.ppermute(send, "core", swap)
    parts = (keep + got.astype(F32)).astype(BF16).reshape(4, z_count // 2, tile, width)
    parts = lax.all_to_all(parts, ("z_lo", "x_lo"), 0, 0, tiled=True)
    parts = pl.pallas_call(
        near_sum_kernel,
        out_shape=jax.ShapeDtypeStruct(parts.shape[1:], BF16),
        in_specs=[VMEM],
        out_specs=VMEM,
        compiler_params=params,
        name="near_sum",
    )(parts)
    parts = lax.all_to_all(parts, "z_hi", 0, 0, tiled=True)

    activations, packed = pl.pallas_call(
        dense_kernel,
        out_shape=(
            jax.ShapeDtypeStruct((tile, width), BF16),
            jax.ShapeDtypeStruct((2 * tile, width), BF16),
        ),
        in_specs=[VMEM] * 4,
        out_specs=(VMEM, VMEM),
        compiler_params=params,
        name="dense",
    )(parts, weight, bias.reshape(1, -1), grad_out)

    gathered = lax.all_gather(packed, "z_hi", axis=0)
    held = jnp.concatenate(
        [gathered[:, :tile], gathered[:, tile:].astype(F32).sum(0, keepdims=True).astype(BF16)], axis=0
    )
    own = lax.all_to_all(jnp.broadcast_to(held[None], (4, *held.shape)), ("z_lo", "x_lo"), 0, 0, tiled=True)
    other = lax.ppermute(own, "core", swap)
    chunks = pl.pallas_call(
        functools.partial(backward_kernel, slots),
        out_shape=jax.ShapeDtypeStruct((near_count, far_count + 1, tile, width), BF16),
        in_specs=[SMEM] * 3 + [VMEM] * 3,
        out_specs=VMEM,
        scratch_shapes=[pltpu.VMEM((4 * z_count + 1, tile, width), BF16)],
        compiler_params=params,
        name="backward",
    )(mine, tile_pos, tile_counts, tiles, own, other)
    parts = lax.all_to_all(chunks, ("y_lo", "x_hi"), 0, 0, tiled=True)
    chunks = pl.pallas_call(
        pack_kernel,
        out_shape=jax.ShapeDtypeStruct((far_count, 2 * tile, width), BF16),
        in_specs=[VMEM],
        out_specs=VMEM,
        compiler_params=params,
        name="pack",
    )(parts)
    parts = lax.all_to_all(chunks, "y_hi", 0, 0, tiled=True)
    grad_features, grad_weight = pl.pallas_call(
        functools.partial(finish_kernel, 1.0 / math.sqrt(nodes)),
        out_shape=(
            jax.ShapeDtypeStruct((tile, width), BF16),
            jax.ShapeDtypeStruct((width, width), F32),
        ),
        in_specs=[VMEM],
        out_specs=(VMEM, VMEM),
        compiler_params=params,
        name="finish",
    )(parts)
    return (activations, grad_weight, grad_features)


def solution(mesh):
    reps, blks = mesh.devices.shape
    fine = Mesh(mesh.devices.reshape(reps // 8, 2, 2, 2, blks // 4, 2, 2), AXES)
    in_specs = (
        P(AXES, None),
        P(),
        P(),
        P(REP, BLK, None, None, None),
        P(REP, BLK, None),
        P(REP, BLK, None),
        P(AXES, None),
    )
    out_specs = (P(AXES, None), P(), P(AXES, None))
    return jax.shard_map(shards, mesh=fine, in_specs=in_specs, out_specs=out_specs, check_vma=False)
```
